128 devices in a mesh: ctx: 32 (over y, z, core), head: 4 (over x).
Axes of the slice: x: 4, y: 4, z: 4, core: 2. Of those that a mesh axis runs over, the one named last changes fastest.
Arguments:
- query_rows: bfloat16 [32768, 4096], P('ctx', 'head'), may hold values from -6 to 6
- key_rows: bfloat16 [32768, 4096], P('ctx', 'head'), may hold values from -6 to 6
- value_rows: bfloat16 [32768, 4096], P('ctx', 'head'), may hold values from -6 to 6
- level_gate: float32 [8, 32, 32768], P(None, 'head', 'ctx'), may hold values from 0 to 2.5, as said below
- out_weight: bfloat16 [4096, 4096], P('head'), may hold values from -0.09375 to 0.09375
Outputs:
- output: bfloat16 [32768, 4096], P(('ctx', 'head'))
The draws below stay inside these ranges and needn't reach their ends.
Inputs may be any that keep to these rules, and one draw needn't show every extreme that they name: `level_gate`: every gate weight is positive.
All inputs are finite; a program needn't handle non-finite values.
Results may differ from the reference program's by a relative error of at most 0.015.
Values may be sent and summed in bfloat16 or wider, within the bound.
No kernel may reach another device: no remote copies, remote signals or barrier semaphores. Data moves between devices by JAX's collectives and lax.ppermute only.
A program may use at most 128 MiB of HBM per device.

```python
import math
import jax
import jax.numpy as jnp
from jax import lax

H = 32
DH = 128
D = 4096
C = 256
LEVELS = 8
SEQ = 32768
N_HEAD = 4


def draw_level_gate(key, part):
    level_ids = jnp.arange(LEVELS, dtype=jnp.float32)[:, None, None]
    base_gate = jnp.exp(jax.random.uniform(key, (LEVELS, H, SEQ), jnp.float32, math.log(0.25), math.log(2.5)))
    return base_gate * jnp.exp(-0.5 * math.log(2.0) * level_ids)


def levels(own_key, dims, pieces, least, high):
    loudness, own = 1.0, jax.random.fold_in(own_key, 6)
    for position, shards_of in pieces:
        steps = jnp.exp(jax.random.uniform(jax.random.fold_in(own, position), (shards_of,), jnp.float32, least / len(pieces), high / len(pieces)))
        loudness = loudness * jnp.repeat(steps, dims[position] // shards_of).reshape([-1 if axis == position else 1 for axis in range(len(dims))])
    return loudness


def scatter_about(key, extent, width, limit, pieces=(), kind=jnp.bfloat16):
    entries = width * jax.random.normal(key, extent, jnp.float32)
    if pieces:
        entries = entries * levels(key, extent, pieces, -0.22, 0.18)
    return jnp.clip(entries, -limit, limit).astype(kind)


def setup_inputs(seed: int = 0) -> dict:
    seeds = jax.random.split(jax.random.key(seed), 6)
    query_rows = scatter_about(seeds[0], (SEQ, H * DH), 1.0, 6.0, ((0, 32), (1, 4)))
    key_rows = scatter_about(seeds[1], (SEQ, H * DH), 1.0, 6.0, ((0, 32), (1, 4)))
    value_rows = scatter_about(seeds[2], (SEQ, H * DH), 1.0, 6.0, ((0, 32), (1, 4)))
    level_gate = draw_level_gate(jax.random.fold_in(seeds[5], 71), 0)
    out_weight = scatter_about(seeds[4], (H * DH, D), (H * DH) ** -0.5, 0.09375, ((0, 4),))
    return {"query_rows": query_rows, "key_rows": key_rows, "value_rows": value_rows, "level_gate": level_gate, "out_weight": out_weight}


EPS = 1e-06

def head_block(query_rows, key_rows, value_rows, level_gate, head_id):
    seq_len = query_rows.shape[0]
    num_stretches = seq_len // C
    col_start = (head_id * DH).astype(jnp.int32)
    query_stretches = lax.dynamic_slice_in_dim(query_rows, col_start, DH, 1).reshape(num_stretches, C, DH).astype(jnp.float32)
    key_stretches = lax.dynamic_slice_in_dim(key_rows, col_start, DH, 1).reshape(num_stretches, C, DH).astype(jnp.float32)
    value_stretches = lax.dynamic_slice_in_dim(value_rows, col_start, DH, 1).reshape(num_stretches, C, DH).astype(jnp.float32)
    gates = lax.dynamic_slice_in_dim(level_gate, head_id.astype(jnp.int32), 1, 1)[:, 0, :].reshape(LEVELS, num_stretches, C)
    scores = jnp.einsum('cti,csi->cts', query_stretches, key_stretches)
    row_ids = lax.broadcasted_iota(jnp.int32, (C, C), 0)
    col_ids = lax.broadcasted_iota(jnp.int32, (C, C), 1)
    weights = (jnp.where(row_ids >= col_ids, scores, 0.0) * gates[0][:, :, None]).astype(jnp.bfloat16)
    combined = jnp.einsum('cts,csj->ctj', weights.astype(jnp.float32), value_stretches)
    stretch_state = jnp.einsum('csi,csj->cij', key_stretches, value_stretches)
    stretch_ids = jnp.arange(num_stretches, dtype=jnp.int32)
    for level_bit in range(LEVELS - 1):
        span_size = 2 ** level_bit
        grouped = stretch_state.reshape(num_stretches // span_size, span_size, DH, DH).sum(axis=1)
        owner_block = stretch_ids // span_size
        bucket = grouped[jnp.maximum(owner_block - 1, 0)].astype(jnp.bfloat16)
        readout = jnp.einsum('cti,cij->ctj', query_stretches, bucket.astype(jnp.float32))
        combined = combined + jnp.where((owner_block % 2 == 1)[:, None, None], readout * gates[level_bit + 1][:, :, None], 0.0)
    normed = combined * lax.rsqrt(lax.optimization_barrier(jnp.mean(combined * combined, axis=-1, keepdims=True)) + EPS)
    return normed.astype(jnp.bfloat16).reshape(seq_len, DH)

def reference(query_rows, key_rows, value_rows, level_gate, out_weight):
    head_ids = jnp.arange(H, dtype=jnp.int32)
    blocks = lax.map(lambda head_id: head_block(query_rows, key_rows, value_rows, level_gate, head_id), head_ids)
    seq_len = query_rows.shape[0]
    normed = jnp.transpose(blocks, (1, 0, 2)).reshape(seq_len, H * DH)
    group_cols = H // N_HEAD * DH
    result = jnp.zeros((seq_len, D), jnp.float32)
    for group_index in range(N_HEAD):
        lower = group_index * group_cols
        upper = lower + group_cols
        partial_value = jnp.dot(normed[:, lower:upper], out_weight[lower:upper], preferred_element_type=jnp.float32)
        partial_value = lax.optimization_barrier(partial_value.astype(jnp.bfloat16)).astype(jnp.float32)
        result = result + partial_value
    return result.astype(jnp.bfloat16)
```

```python
import jax
import jax.numpy as jnp
from jax import lax
from jax.experimental import pallas as pl
from jax.experimental.pallas import tpu as pltpu
from jax.sharding import PartitionSpec as P

C = 256
DH = 128
EPS = 1e-06
BF = jnp.bfloat16
F32 = jnp.float32


def state_kernel(k_ref, v_ref, total_ref, local_ref):
    for head in range(2):
        cols = slice(head * DH, (head + 1) * DH)
        states = []
        for stretch in range(4):
            rows = slice(stretch * C, (stretch + 1) * C)
            states.append(
                lax.dot_general(
                    k_ref[rows, cols],
                    v_ref[rows, cols],
                    (((0,), (0,)), ((), ())),
                    preferred_element_type=F32,
                )
            )
        first_two = states[0] + states[1]
        total_ref[head] = (first_two + states[2] + states[3]).astype(BF)
        local_ref[head, 0] = states[0].astype(BF)
        local_ref[head, 1] = states[2].astype(BF)
        local_ref[head, 2] = first_two.astype(BF)


def local_kernel(q_ref, k_ref, v_ref, g_ref, local_ref, out_ref):
    pair = pl.program_id(0)
    rows_ids = lax.broadcasted_iota(jnp.int32, (C, C), 0)
    cols_ids = lax.broadcasted_iota(jnp.int32, (C, C), 1)
    causal = rows_ids >= cols_ids
    for stretch in range(4):
        rows = slice(stretch * C, (stretch + 1) * C)
        for head in range(2):
            cols = slice(head * DH, (head + 1) * DH)
            q = q_ref[rows, cols]
            scores = lax.dot_general(
                q, k_ref[rows, cols], (((1,), (1,)), ((), ())), preferred_element_type=F32
            )
            weights = jnp.where(causal, scores, 0.0).astype(BF)
            gate = lambda level: g_ref[0, rows, head * 8 + level : head * 8 + level + 1]
            out = jnp.dot(weights, v_ref[rows, cols], preferred_element_type=F32) * gate(0)
            parts, states = [], []
            if stretch % 2 == 1:
                parts.append(q * gate(1).astype(BF))
                states.append(local_ref[head, stretch // 2])
            if stretch // 2 == 1:
                parts.append(q * gate(2).astype(BF))
                states.append(local_ref[head, 2])
            if parts:
                out = out + jnp.dot(
                    jnp.concatenate(parts, 1), jnp.concatenate(states, 0), preferred_element_type=F32
                )
            out_ref[rows, cols] = out


def far_kernel(q_ref, comb_ref, g_ref, far_ref, out_ref):
    levels = far_ref.shape[0]
    for stretch in range(4):
        rows = slice(stretch * C, (stretch + 1) * C)
        for head in range(2):
            cols = slice(head * DH, (head + 1) * DH)
            q = q_ref[rows, cols]
            parts = [
                q * g_ref[0, rows, head * 8 + 3 + j : head * 8 + 4 + j].astype(BF)
                for j in range(levels)
            ]
            states = jnp.concatenate([far_ref[j, head] for j in range(levels)], 0)
            out = comb_ref[rows, cols] + jnp.dot(
                jnp.concatenate(parts, 1), states, preferred_element_type=F32
            )
            mean = jnp.mean(out * out, axis=-1, keepdims=True)
            out_ref[rows, cols] = (out * lax.rsqrt(mean + EPS)).astype(BF)


def on_device(query_rows, key_rows, value_rows, level_gate, out_weight):
    tokens, width = query_rows.shape
    levels, heads, _ = level_gate.shape
    ctx_size = lax.axis_size("ctx")
    ctx_bits = ctx_size.bit_length() - 1
    pairs = heads // 2
    me = lax.axis_index("ctx")

    wide = pl.BlockSpec((tokens, 2 * DH), lambda p: (0, p))
    state_shape = lambda *lead: pl.BlockSpec((2, *lead, DH, DH), lambda p: (p,) + (0,) * (len(lead) + 2))
    total, local = pl.pallas_call(
        state_kernel,
        grid=(pairs,),
        in_specs=[wide, wide],
        out_specs=[state_shape(), state_shape(3)],
        out_shape=[
            jax.ShapeDtypeStruct((heads, DH, DH), BF),
            jax.ShapeDtypeStruct((heads, 3, DH, DH), BF),
        ],
        cost_estimate=pl.CostEstimate(flops=2 * tokens * width * DH, bytes_accessed=5 << 20, transcendentals=0),
        compiler_params=pltpu.CompilerParams(vmem_limit_bytes=32 << 20),
        name="states",
    )(key_rows, value_rows)

    far = []
    for bit in range(ctx_bits):
        step = 1 << bit
        got = lax.ppermute(total, "ctx", [(i, i ^ step) for i in range(ctx_size)])
        mine = (me // step) % 2 == 1
        far.append(jnp.where(mine, got, jnp.zeros_like(got)))
        total = (total.astype(F32) + got.astype(F32)).astype(BF)
    far = jnp.stack(far)

    gates = jnp.transpose(level_gate.reshape(levels, pairs, 2, tokens), (1, 3, 2, 0)).reshape(
        pairs, tokens, 2 * levels
    )
    gate_spec = pl.BlockSpec((1, tokens, 2 * levels), lambda p: (p, 0, 0))
    combined = pl.pallas_call(
        local_kernel,
        grid=(pairs,),
        in_specs=[wide, wide, wide, gate_spec, state_shape(3)],
        out_specs=wide,
        out_shape=jax.ShapeDtypeStruct((tokens, width), F32),
        cost_estimate=pl.CostEstimate(flops=12 * tokens * width * DH, bytes_accessed=12 << 20, transcendentals=0),
        compiler_params=pltpu.CompilerParams(vmem_limit_bytes=32 << 20),
        name="local",
    )(query_rows, key_rows, value_rows, gates, local)

    normed = pl.pallas_call(
        far_kernel,
        grid=(pairs,),
        in_specs=[
            wide,
            wide,
            gate_spec,
            pl.BlockSpec((ctx_bits, 2, DH, DH), lambda p: (0, p, 0, 0)),
        ],
        out_specs=wide,
        out_shape=jax.ShapeDtypeStruct((tokens, width), BF),
        cost_estimate=pl.CostEstimate(flops=10 * tokens * width * DH, bytes_accessed=9 << 20, transcendentals=0),
        compiler_params=pltpu.CompilerParams(vmem_limit_bytes=32 << 20),
        name="far_norm",
    )(query_rows, combined, gates, far)

    partial = jnp.dot(normed, out_weight, preferred_element_type=F32).astype(BF)
    return lax.psum_scatter(partial, "head", scatter_dimension=0, tiled=True)


def solution(mesh):
    in_specs = (
        P("ctx", "head"),
        P("ctx", "head"),
        P("ctx", "head"),
        P(None, "head", "ctx"),
        P("head", None),
    )
    out_specs = P(("ctx", "head"), None)
    return jax.shard_map(
        on_device, mesh=mesh, in_specs=in_specs, out_specs=out_specs, check_vma=False
    )
```

```python
import jax
import jax.numpy as jnp
from jax import lax
from jax.experimental import pallas as pl
from jax.experimental.pallas import tpu as pltpu
from jax.sharding import PartitionSpec as P

C = 256
DH = 128
EPS = 1e-06
BF = jnp.bfloat16
F32 = jnp.float32
VMEM_LIMIT = 56 << 20
CHUNKS = 4


def dot_t(a, b):
    return lax.dot_general(a, b, (((1,), (1,)), ((), ())), preferred_element_type=F32)


def dot_tt(a, b):
    return lax.dot_general(a, b, (((0,), (0,)), ((), ())), preferred_element_type=F32)


def params():
    return pltpu.CompilerParams(vmem_limit_bytes=VMEM_LIMIT)


def cost(flops, nbytes):
    return pl.CostEstimate(flops=flops, bytes_accessed=nbytes, transcendentals=0)


def state_kernel(k_ref, v_ref, total_ref, local_ref):
    for head in range(2):
        cols = slice(head * DH, (head + 1) * DH)
        states = []
        for stretch in range(4):
            rows = slice(stretch * C, (stretch + 1) * C)
            states.append(dot_tt(v_ref[rows, cols], k_ref[rows, cols]))
        first_two = states[0] + states[1]
        total_ref[head] = (first_two + states[2] + states[3]).astype(BF)
        local_ref[head, 0] = states[0].astype(BF)
        local_ref[head, 1] = states[2].astype(BF)
        local_ref[head, 2] = first_two.astype(BF)


def local_kernel(q_ref, k_ref, v_ref, g_ref, local_ref, out_ref):
    pair = pl.program_id(0)
    causal = lax.broadcasted_iota(jnp.int32, (C, C), 0) <= lax.broadcasted_iota(
        jnp.int32, (C, C), 1
    )
    for stretch in range(4):
        rows = slice(stretch * C, (stretch + 1) * C)
        for head in range(2):
            cols = slice(head * DH, (head + 1) * DH)
            q = q_ref[rows, cols]
            gate = lambda level: g_ref[level, pl.ds(2 * pair + head, 1), rows]
            weights = jnp.where(causal, dot_t(k_ref[rows, cols], q), 0.0).astype(BF)
            out = dot_tt(v_ref[rows, cols], weights) * gate(0)
            if stretch % 2 == 1:
                out = out + dot_t(local_ref[head, stretch // 2], q) * gate(1)
            if stretch // 2 == 1:
                out = out + dot_t(local_ref[head, 2], q) * gate(2)
            out_ref[cols, rows] = out


def far_kernel(s_ref, q_ref, comb_ref, g_ref, sib_ref, zo_ref, zs_ref, yo_ref, ys_ref, out_ref):
    core = s_ref[0]
    masks = [s_ref[1 + j].astype(F32) for j in range(5)]
    for slot in range(8):
        own = slot < 4
        inner = slot % 4
        head = (core if own else 1 - core) * 4 + inner
        z_ref, y_ref = (zo_ref, yo_ref) if own else (zs_ref, ys_ref)
        offset = pl.multiple_of(head * DH, DH)
        q = q_ref[:, pl.ds(offset, DH)]
        out = comb_ref[pl.ds(offset, DH), :]
        states = [sib_ref[head], z_ref[0, inner], z_ref[1, inner], y_ref[0, inner], y_ref[1, inner]]
        for j in range(5):
            out = out + dot_t(states[j], q) * (g_ref[3 + j, pl.ds(head, 1), :] * masks[j])
        mean = jnp.mean(out * out, axis=0, keepdims=True)
        out_ref[0, :, pl.ds(offset, DH)] = jnp.transpose(out * lax.rsqrt(mean + EPS)).astype(BF)


def proj_kernel(s_ref, own_ref, got_ref, w_ref, a_ref, b_ref, c_ref, d_ref, out_ref):
    acc = jnp.dot(own_ref[0], w_ref[...], preferred_element_type=F32)
    for piece, ref in enumerate((a_ref, b_ref, c_ref, d_ref)):
        cols = pl.ds(pl.multiple_of(s_ref[piece] * 256, 256), 256)
        acc = acc + jnp.dot(got_ref[0, :, cols], ref[...], preferred_element_type=F32)
    out_ref[...] = acc.astype(out_ref.dtype)


def on_device(query_rows, key_rows, value_rows, level_gate, out_weight):
    tokens, width = query_rows.shape
    levels, heads, _ = level_gate.shape
    model = out_weight.shape[1]
    pairs = heads // 2
    ctx_size = lax.axis_size("ctx")
    me = lax.axis_index("ctx")
    x = lax.axis_index("head")
    bit = lambda j: lax.bitwise_and(lax.shift_right_logical(me, j), 1)
    core = bit(0)

    def ctx_swap(array, step):
        return lax.ppermute(array, "ctx", [(i, i ^ step) for i in range(ctx_size)])

    def near(array):
        return lax.ppermute(array, "head", [(i, i ^ 1) for i in range(4)])

    def across(array):
        return lax.ppermute(array, "head", [(i, 3 - i) for i in range(4)])

    chunk = model // CHUNKS
    pieces, orders = [], []
    for i in range(CHUNKS):
        step_bit = 1 if i % 2 == 0 else 3
        quarter = core * 2 + bit(step_bit)
        other = core * 2 + 1 - bit(step_bit)
        mine = near(lax.dynamic_slice(out_weight, (quarter * 256, i * chunk), (256, chunk)))
        next_one = ctx_swap(mine, 1 << step_bit)
        pieces.append((mine, next_one, ctx_swap(mine, 1), ctx_swap(next_one, 1)))
        flip = lambda part: lax.bitwise_xor(part, 2)
        orders.append(jnp.stack([quarter, other, flip(quarter), flip(other)]).astype(jnp.int32))

    wide = pl.BlockSpec((tokens, 2 * DH), lambda p: (0, p))
    total, local = pl.pallas_call(
        state_kernel,
        grid=(pairs,),
        in_specs=[wide, wide],
        out_specs=[
            pl.BlockSpec((2, DH, DH), lambda p: (p, 0, 0)),
            pl.BlockSpec((2, 3, DH, DH), lambda p: (p, 0, 0, 0)),
        ],
        out_shape=[
            jax.ShapeDtypeStruct((heads, DH, DH), BF),
            jax.ShapeDtypeStruct((heads, 3, DH, DH), BF),
        ],
        cost_estimate=cost(2 * tokens * width * DH, 5 << 20),
        compiler_params=params(),
        name="states",
    )(key_rows, value_rows)

    half = heads // 2
    pick = lambda array: lax.dynamic_slice_in_dim(array, core * half, half, 0)
    add = lambda *arrays: sum(a.astype(F32) for a in arrays)
    sibling = ctx_swap(total, 1)
    chip = add(pick(total), pick(sibling)).astype(BF)
    z1, z2, z3 = (ctx_swap(chip, step) for step in (2, 4, 6))
    z_own = jnp.stack([z1, add(z2, z3).astype(BF)])
    row = add(chip, z1, z2, z3).astype(BF)
    y1, y2, y3 = (ctx_swap(row, step) for step in (8, 16, 24))
    z_sib = ctx_swap(z_own, 1)
    y_own = jnp.stack([y1, add(y2, y3).astype(BF)])
    y_sib = ctx_swap(y_own, 1)

    combined = pl.pallas_call(
        local_kernel,
        grid=(pairs,),
        in_specs=[
            wide,
            wide,
            wide,
            pl.BlockSpec((levels, heads, tokens), lambda p: (0, 0, 0)),
            pl.BlockSpec((2, 3, DH, DH), lambda p: (p, 0, 0, 0)),
        ],
        out_specs=pl.BlockSpec((2 * DH, tokens), lambda p: (p, 0)),
        out_shape=jax.ShapeDtypeStruct((width, tokens), F32),
        cost_estimate=cost(12 * tokens * width * DH, 12 << 20),
        compiler_params=params(),
        name="local",
    )(query_rows, key_rows, value_rows, level_gate, local)

    def far_norm(blocks, name):
        count = len(blocks)
        scalars = jnp.stack([core] + [bit(j) for j in range(5)] + list(blocks)).astype(jnp.int32)
        full = lambda *shape: pl.BlockSpec(shape, lambda i, s: (0,) * len(shape))
        return pl.pallas_call(
            far_kernel,
            grid_spec=pltpu.PrefetchScalarGridSpec(
                num_scalar_prefetch=1,
                grid=(count,),
                in_specs=[
                    pl.BlockSpec((C, width), lambda i, s: (s[6 + i], 0)),
                    pl.BlockSpec((width, C), lambda i, s: (0, s[6 + i])),
                    pl.BlockSpec((levels, heads, C), lambda i, s: (0, 0, s[6 + i])),
                    full(heads, DH, DH),
                    full(2, half, DH, DH),
                    full(2, half, DH, DH),
                    full(2, half, DH, DH),
                    full(2, half, DH, DH),
                ],
                out_specs=pl.BlockSpec((1, C, width), lambda i, s: (i, 0, 0)),
            ),
            out_shape=jax.ShapeDtypeStruct((count, C, width), BF),
            cost_estimate=cost(10 * count * C * width * DH, count * (2 << 20)),
            compiler_params=params(),
            name=name,
        )(scalars, query_rows, combined, level_gate, sibling, z_own, z_sib, y_own, y_sib)

    near_x = lax.bitwise_xor(x, 1)
    across_x = 3 - x
    far_x = lax.bitwise_xor(x, 2)
    first = far_norm([far_x], "far_first")
    got_across = near(first)
    rest = far_norm([across_x, near_x, x], "far_rest")
    got_own = near(rest[1:2])

    tile = 256
    tiles = chunk // tile

    def project(own_index, got, i, dtype, name):
        piece = pl.BlockSpec((256, tile), lambda n, s: (0, n))
        return pl.pallas_call(
            proj_kernel,
            grid_spec=pltpu.PrefetchScalarGridSpec(
                num_scalar_prefetch=1,
                grid=(tiles,),
                in_specs=[
                    pl.BlockSpec((1, C, width), lambda n, s: (own_index, 0, 0)),
                    pl.BlockSpec((1, C, width), lambda n, s: (0, 0, 0)),
                    pl.BlockSpec((width, tile), lambda n, s: (0, i * tiles + n)),
                    piece,
                    piece,
                    piece,
                    piece,
                ],
                out_specs=pl.BlockSpec((C, tile), lambda n, s: (0, n)),
            ),
            out_shape=jax.ShapeDtypeStruct((C, chunk), dtype),
            cost_estimate=cost(4 * C * width * chunk, 5 << 20),
            compiler_params=params(),
            name=name,
        )(orders[i], rest, got, out_weight, *pieces[i])

    received = []
    for i in range(CHUNKS):
        received.append(across(project(0, got_across, i, BF, "proj_across%d" % i)))
    outs = []
    for i in range(CHUNKS):
        own = project(2, got_own, i, F32, "proj_own%d" % i)
        outs.append((own + received[i].astype(F32)).astype(BF))
    return jnp.concatenate(outs, 1)


def solution(mesh):
    in_specs = (
        P("ctx", "head"),
        P("ctx", "head"),
        P("ctx", "head"),
        P(None, "head", "ctx"),
        P("head", None),
    )
    out_specs = P(("ctx", "head"), None)
    return jax.shard_map(
        on_device, mesh=mesh, in_specs=in_specs, out_specs=out_specs, check_vma=False
    )
```

```python
import functools

import jax
import jax.numpy as jnp
from jax import lax
from jax.experimental import pallas as pl
from jax.experimental.pallas import tpu as pltpu
from jax.sharding import PartitionSpec as P

C = 256
DH = 128
EPS = 1e-06
BF = jnp.bfloat16
F32 = jnp.float32
VMEM_LIMIT = 36 << 20
CHUNKS = 4
STEP_BITS = (1, 3, 1, 3)


def dot_t(a, b):
    return lax.dot_general(a, b, (((1,), (1,)), ((), ())), preferred_element_type=F32)


def dot_tt(a, b):
    return lax.dot_general(a, b, (((0,), (0,)), ((), ())), preferred_element_type=F32)


def params():
    return pltpu.CompilerParams(vmem_limit_bytes=VMEM_LIMIT)


def cost(flops, nbytes):
    return pl.CostEstimate(flops=flops >> 12, bytes_accessed=nbytes >> 12, transcendentals=0)


def start_all(copies):
    for copy in copies:
        copy.start()
    return copies


def start_all(copies):
    for copy in copies:
        copy.start()
    return copies


def wait_all(copies):
    for copy in copies:
        copy.wait()


def slice_copies(chunks, s_ref, w_hbm, outs, sems, first):
    copies = []
    for n, (chunk, out) in enumerate(zip(chunks, outs)):
        rows, cols = out.shape
        start = (s_ref[0] * 2 + s_ref[1 + STEP_BITS[chunk]]) * rows
        src = w_hbm.at[pl.ds(pl.multiple_of(start, rows), rows), chunk * cols : (chunk + 1) * cols]
        copies.append(pltpu.make_async_copy(src, out, sems.at[first + n]))
    return copies


def state_kernel(
    s_ref, k_hbm, v_hbm, w_hbm, total_ref, local_ref, w0_hbm, w1_hbm, k_buf, v_buf, acc, sems
):
    heads = total_ref.shape[0]
    copies = []
    for stretch in range(4):
        rows = slice(stretch * C, (stretch + 1) * C)
        copies.append(
            start_all(
                [
                    pltpu.make_async_copy(src.at[rows], dst.at[rows], sems.at[2 * stretch + n])
                    for n, (src, dst) in enumerate(((k_hbm, k_buf), (v_hbm, v_buf)))
                ]
            )
        )
    slices = start_all(slice_copies((0, 1), s_ref, w_hbm, (w0_hbm, w1_hbm), sems, 8))
    for stretch in range(4):
        rows = slice(stretch * C, (stretch + 1) * C)
        wait_all(copies[stretch])
        for head in range(heads):
            cols = slice(head * DH, (head + 1) * DH)
            state = dot_tt(v_buf[rows, cols], k_buf[rows, cols])
            if stretch == 0:
                acc[head] = state
                local_ref[head, 0] = state.astype(BF)
            elif stretch == 1:
                state = acc[head] + state
                acc[head] = state
                local_ref[head, 2] = state.astype(BF)
            elif stretch == 2:
                acc[head] = acc[head] + state
                local_ref[head, 1] = state.astype(BF)
            else:
                total_ref[head] = (acc[head] + state).astype(BF)
    wait_all(slices)


def local_kernel(
    s_ref, q_hbm, k_hbm, v_hbm, w_hbm, g_ref, local_ref, token_ref, out_hbm, w2_ref, w3_ref,
    q_buf, k_buf, v_buf, out_buf, sems
):
    copies = []
    for stretch in range(4):
        rows = slice(stretch * C, (stretch + 1) * C)
        copies.append(
            start_all(
                [
                    pltpu.make_async_copy(src.at[rows], dst.at[rows], sems.at[3 * stretch + n])
                    for n, (src, dst) in enumerate(
                        ((q_hbm, q_buf), (k_hbm, k_buf), (v_hbm, v_buf))
                    )
                ]
            )
        )
    slices = start_all(slice_copies((2, 3), s_ref, w_hbm, (w2_ref, w3_ref), sems, 16))
    causal = lax.broadcasted_iota(jnp.int32, (C, C), 0) <= lax.broadcasted_iota(
        jnp.int32, (C, C), 1
    )
    stores = []
    for stretch in range(4):
        rows = slice(stretch * C, (stretch + 1) * C)
        wait_all(copies[stretch])
        for head in range(local_ref.shape[0]):
            cols = slice(head * DH, (head + 1) * DH)
            gate = lambda level: g_ref[level, head : head + 1, rows]
            q = q_buf[rows, cols]
            weights = jnp.where(causal, dot_t(k_buf[rows, cols], q), 0.0).astype(BF)
            out = dot_tt(v_buf[rows, cols], weights) * gate(0)
            if stretch % 2 == 1:
                out = out + dot_t(local_ref[head, stretch // 2], q) * gate(1)
            if stretch // 2 == 1:
                out = out + dot_t(local_ref[head, 2], q) * gate(2)
            out_buf[stretch, cols, :] = out
        store = pltpu.make_async_copy(
            out_buf.at[stretch], out_hbm.at[stretch], sems.at[12 + stretch]
        )
        store.start()
        stores.append(store)
    wait_all(stores)
    wait_all(slices)


def far_block(s_ref, q_ref, comb_ref, g_ref, core_ref, zo_ref, yo_ref, zs_ref, ys_ref, out_ref):
    masks = [s_ref[1 + j].astype(F32) for j in range(5)]
    half = zo_ref.shape[1]
    for slot in range(2 * half):
        own = slot < half
        inner = slot % half
        head = (s_ref[0] if own else 1 - s_ref[0]) * half + inner
        z_ref, y_ref = (zo_ref, yo_ref) if own else (zs_ref, ys_ref)
        offset = pl.multiple_of(head * DH, DH)
        states = jnp.concatenate(
            [core_ref[head], z_ref[0, inner], z_ref[1, inner], y_ref[0, inner], y_ref[1, inner]], 0
        )
        read = dot_t(states, q_ref[:, pl.ds(offset, DH)])
        out = comb_ref[0, pl.ds(offset, DH), :]
        for j in range(5):
            out = out + read[j * DH : (j + 1) * DH] * (g_ref[3 + j, pl.ds(head, 1), :] * masks[j])
        mean = jnp.mean(out * out, axis=0, keepdims=True)
        out_ref[:, slot * DH : (slot + 1) * DH] = jnp.transpose(
            (out * lax.rsqrt(mean + EPS)).astype(BF)
        )


def far_first_kernel(s_ref, token_ref, *refs):
    far_block(s_ref, *refs)


def far_rest_kernel(s_ref, token_ref, *refs):
    *inputs, near_ref, keep_ref, buf = refs
    far_block(s_ref, *inputs, buf)

    @pl.when(pl.program_id(0) == 0)
    def _():
        near_ref[...] = buf[...]

    @pl.when(pl.program_id(0) > 0)
    def _():
        keep_ref[0] = buf[...]


def gate_kernel(data_ref, token_ref, out_ref):
    pass


def weight_copies(chunk, s_ref, w_hbm, pieces, dst, size, cols, sems, first):
    rows = dst.shape[0]
    half, quarter = rows // 4, rows // 8
    core, low = s_ref[0], s_ref[1 + STEP_BITS[chunk]]
    copies = []

    def add(src, row, count):
        copies.append(
            pltpu.make_async_copy(
                src, dst.at[pl.ds(row, count), cols], sems.at[first + len(copies)]
            )
        )

    own_cols = slice(chunk * size + cols.start, chunk * size + cols.stop)
    for part, which in enumerate((core, 1 - core)):
        add(w_hbm.at[pl.ds(pl.multiple_of(which * half, half), half), own_cols], part * half, half)
    for part, ref in enumerate(pieces):
        place = low if part % 2 == 0 else 1 - low
        start = pl.multiple_of((2 + part // 2) * half + place * quarter, quarter)
        add(ref.at[:, cols], start, quarter)
    return copies


def across_kernel(chunk, s_ref, token_ref, keep, got, w_hbm, *refs):
    pieces, out_ref, lhs, w, sems = refs[:4], *refs[4:]
    width = lhs.shape[1] // 2
    size = out_ref.shape[1]
    tile = size // 2
    left = start_all(
        [
            pltpu.make_async_copy(keep.at[0], lhs.at[:, :width], sems.at[0]),
            pltpu.make_async_copy(got, lhs.at[:, width:], sems.at[1]),
        ]
    )
    right = [
        start_all(
            weight_copies(
                chunk, s_ref, w_hbm, pieces, w, size, slice(n * tile, (n + 1) * tile), sems, 2 + 6 * n
            )
        )
        for n in range(2)
    ]
    wait_all(left)
    for n, group in enumerate(right):
        cols = slice(n * tile, (n + 1) * tile)
        wait_all(group)
        out_ref[:, cols] = jnp.dot(lhs[...], w[:, cols], preferred_element_type=F32).astype(
            out_ref.dtype
        )


def own_kernel(s_ref, token_ref, keep, got, w_hbm, *refs):
    count = CHUNKS
    pieces = [refs[4 * i : 4 * i + 4] for i in range(count)]
    received = refs[4 * count : 5 * count - 1]
    out_hbm, last_ref, lhs, w, out_buf, sems = refs[5 * count - 1 :]
    width = lhs.shape[1] // 2
    size = w.shape[2]
    left = start_all(
        [
            pltpu.make_async_copy(keep.at[1], lhs.at[:, :width], sems.at[0]),
            pltpu.make_async_copy(got, lhs.at[:, width:], sems.at[1]),
        ]
    )
    right = [
        start_all(
            weight_copies(
                i, s_ref, w_hbm, pieces[i], w.at[i], size, slice(0, size), sems, 2 + 6 * i
            )
        )
        for i in range(count)
    ]
    wait_all(left)
    stores = []
    for i in range(count):
        cols = slice(i * size, (i + 1) * size)
        wait_all(right[i])
        own = jnp.dot(lhs[...], w[i], preferred_element_type=F32)
        if i == count - 1:
            last_ref[...] = own
            break
        out_buf[:, cols] = (own + received[i][...].astype(F32)).astype(BF)
        store = pltpu.make_async_copy(
            out_buf.at[:, cols], out_hbm.at[:, cols], sems.at[2 + 6 * count + i]
        )
        store.start()
        stores.append(store)
    wait_all(stores)


def finish_kernel(base_ref, own_ref, got_ref, out_hbm, buf, sem):
    buf[...] = (own_ref[...] + got_ref[...].astype(F32)).astype(BF)
    size = buf.shape[1]
    copy = pltpu.make_async_copy(buf, out_hbm.at[:, (CHUNKS - 1) * size : CHUNKS * size], sem.at[0])
    copy.start()
    copy.wait()


def on_device(query_rows, key_rows, value_rows, level_gate, out_weight):
    tokens, width = query_rows.shape
    levels, heads, _ = level_gate.shape
    model = out_weight.shape[1]
    stretches = tokens // C
    half = heads // 2
    chunk = model // CHUNKS
    ctx_size = lax.axis_size("ctx")
    me = lax.axis_index("ctx")
    x = lax.axis_index("head")
    bit = lambda j: lax.bitwise_and(lax.shift_right_logical(me, j), 1)
    core = bit(0)
    any_spec = pl.BlockSpec(memory_space=pl.ANY)
    vmem_spec = pl.BlockSpec(memory_space=pltpu.VMEM)
    smem_spec = pl.BlockSpec(memory_space=pltpu.SMEM)
    dma = pltpu.SemaphoreType.DMA
    near_x, across_x, far_x = lax.bitwise_xor(x, 1), 3 - x, lax.bitwise_xor(x, 2)
    scalars = jnp.stack([core] + [bit(j) for j in range(5)] + [far_x, near_x, across_x, x])
    scalars = scalars.astype(jnp.int32)
    hbm = lambda array: pltpu.with_memory_space_constraint(array, pltpu.HBM)
    query_rows, key_rows, value_rows, out_weight = map(
        hbm, (query_rows, key_rows, value_rows, out_weight)
    )

    def ctx_swap(array, step):
        return lax.ppermute(array, "ctx", [(i, i ^ step) for i in range(ctx_size)])

    def near(array):
        return lax.ppermute(array, "head", [(i, i ^ 1) for i in range(4)])

    def across(array):
        return lax.ppermute(array, "head", [(i, 3 - i) for i in range(4)])

    def after(array, token):
        return pl.pallas_call(
            gate_kernel,
            in_specs=[any_spec, any_spec],
            out_specs=any_spec,
            out_shape=jax.ShapeDtypeStruct(array.shape, array.dtype),
            input_output_aliases={0: 0},
            name="after",
        )(array, token)

    piece_shape = jax.ShapeDtypeStruct((width // 4, chunk), BF)
    total, local, slice0, slice1 = pl.pallas_call(
        state_kernel,
        in_specs=[smem_spec, any_spec, any_spec, any_spec],
        out_specs=[vmem_spec] * 4,
        out_shape=[
            jax.ShapeDtypeStruct((heads, DH, DH), BF),
            jax.ShapeDtypeStruct((heads, 3, DH, DH), BF),
            piece_shape,
            piece_shape,
        ],
        scratch_shapes=[
            pltpu.VMEM((tokens, width), BF),
            pltpu.VMEM((tokens, width), BF),
            pltpu.VMEM((heads, DH, DH), F32),
            dma((10,)),
        ],
        cost_estimate=cost(2 * tokens * width * DH, 7 << 20),
        compiler_params=params(),
        name="states",
    )(scalars, key_rows, value_rows, out_weight)

    pick = lambda array: lax.dynamic_slice_in_dim(array, core * half, half, 0)
    add = lambda *arrays: sum(a.astype(F32) for a in arrays)
    sibling = ctx_swap(total, 1)
    fetched = [near(slice0)]
    chip = add(pick(total), pick(sibling)).astype(BF)
    z1, z2, z3 = (ctx_swap(chip, step) for step in (2, 4, 6))
    fetched.append(near(after(slice1, chip)))

    combined, slice2, slice3 = pl.pallas_call(
        local_kernel,
        in_specs=[smem_spec] + [any_spec] * 4 + [vmem_spec] * 2 + [any_spec],
        out_specs=[any_spec, vmem_spec, vmem_spec],
        out_shape=[pltpu.HBM((stretches, width, C), F32), piece_shape, piece_shape],
        scratch_shapes=[
            pltpu.VMEM((tokens, width), BF),
            pltpu.VMEM((tokens, width), BF),
            pltpu.VMEM((tokens, width), BF),
            pltpu.VMEM((stretches, width, C), F32),
            dma((18,)),
        ],
        cost_estimate=cost(12 * tokens * width * DH, 12 << 20),
        compiler_params=params(),
        name="local",
    )(scalars, query_rows, key_rows, value_rows, out_weight, level_gate, local, chip)
    z3 = after(z3, combined)
    z_own = jnp.stack([z1, add(z2, z3).astype(BF)])
    row = add(chip, z1, z2, z3).astype(BF)
    y1, y2, y3 = (ctx_swap(row, step) for step in (8, 16, 24))
    z_sib = ctx_swap(z_own, 1)

    def gather(i, first_token, second_token):
        mine = after(fetched[i], first_token)
        other = after(ctx_swap(mine, 1 << STEP_BITS[i]), second_token)
        return (mine, other, ctx_swap(mine, 1), ctx_swap(other, 1))

    y_own = jnp.stack([y1, add(y2, y3).astype(BF)])
    y_sib = ctx_swap(y_own, 1)
    fetched.append(near(after(slice2, z_own)))
    pieces = [gather(0, z_own, y_own)]

    def far_norm(first, token):
        count = 1 if first else 3
        base = 6 if first else 7
        block = (C, width)
        return pl.pallas_call(
            far_first_kernel if first else far_rest_kernel,
            grid_spec=pltpu.PrefetchScalarGridSpec(
                num_scalar_prefetch=1,
                grid=(count,),
                in_specs=[
                    any_spec,
                    pl.BlockSpec((C, width), lambda i, s: (s[base + i], 0)),
                    pl.BlockSpec((1, width, C), lambda i, s: (s[base + i], 0, 0)),
                    pl.BlockSpec((levels, heads, C), lambda i, s: (0, 0, s[base + i])),
                ]
                + [vmem_spec] * 5,
                out_specs=[pl.BlockSpec(block, lambda i, s: (0, 0))]
                + (
                    []
                    if first
                    else [pl.BlockSpec((1, *block), lambda i, s: (jnp.maximum(i - 1, 0), 0, 0))]
                ),
                scratch_shapes=[] if first else [pltpu.VMEM(block, BF)],
            ),
            out_shape=[pltpu.HBM(block, BF)] + ([] if first else [pltpu.HBM((2, *block), BF)]),
            cost_estimate=cost(10 * count * C * width * DH, count * (2 << 20)),
            compiler_params=params(),
            name="far_first" if first else "far_rest",
        )(
            scalars, token, query_rows, combined, level_gate, sibling, z_own, y_own, z_sib, y_sib
        )

    (first,) = far_norm(True, pieces[0][3])
    got_across = near(first)
    near_rows, keep = far_norm(False, first)

    def project(i, tokens):
        def kernel(s_ref, *refs):
            across_kernel(i, s_ref, *refs[len(tokens) - 1 :])

        return pl.pallas_call(
            kernel,
            in_specs=[smem_spec] + [any_spec] * (7 + len(tokens)),
            out_specs=vmem_spec,
            out_shape=jax.ShapeDtypeStruct((C, chunk), BF),
            scratch_shapes=[
                pltpu.VMEM((C, 2 * width), BF),
                pltpu.VMEM((2 * width, chunk), BF),
                dma((14,)),
            ],
            cost_estimate=cost(4 * C * width * chunk, 5 << 20),
            compiler_params=params(),
            name="across%d" % i,
        )(scalars, *tokens, keep, got_across, out_weight, *pieces[i])

    partials = [project(0, [keep])]
    received = [across(partials[0])]
    pieces.append(gather(1, y_own, keep))
    fetched.append(near(after(slice3, partials[0])))
    pieces.append(gather(2, keep, partials[0]))
    partials.append(project(1, [partials[0]]))
    received.append(across(partials[1]))
    got_own = near(after(near_rows, partials[1]))
    partials.append(project(2, [partials[1], received[0]]))
    received.append(across(partials[2]))
    pieces.append(gather(3, partials[1], partials[2]))
    partials.append(project(3, [partials[2], received[1]]))
    received.append(across(partials[3]))
    token = partials[3]
    out, last = pl.pallas_call(
        own_kernel,
        in_specs=[smem_spec] + [any_spec] * (4 + 4 * CHUNKS) + [vmem_spec] * (CHUNKS - 1),
        out_specs=[any_spec, vmem_spec],
        out_shape=[pltpu.HBM((C, model), BF), jax.ShapeDtypeStruct((C, chunk), F32)],
        scratch_shapes=[
            pltpu.VMEM((C, 2 * width), BF),
            pltpu.VMEM((CHUNKS, 2 * width, chunk), BF),
            pltpu.VMEM((C, (CHUNKS - 1) * chunk), BF),
            dma((2 + 7 * CHUNKS,)),
        ],
        cost_estimate=cost(4 * C * width * model, 20 << 20),
        compiler_params=params(),
        name="own",
    )(
        scalars,
        token,
        keep,
        got_own,
        out_weight,
        *[piece for group in pieces for piece in group],
        *received[:-1],
    )
    return pl.pallas_call(
        finish_kernel,
        in_specs=[any_spec, vmem_spec, vmem_spec],
        out_specs=any_spec,
        out_shape=pltpu.HBM((C, model), BF),
        scratch_shapes=[pltpu.VMEM((C, chunk), BF), dma((1,))],
        input_output_aliases={0: 0},
        compiler_params=params(),
        name="finish",
    )(out, last, received[-1])


def solution(mesh):
    in_specs = (
        P("ctx", "head"),
        P("ctx", "head"),
        P("ctx", "head"),
        P(None, "head", "ctx"),
        P("head", None),
    )
    out_specs = P(("ctx", "head"), None)
    return jax.shard_map(
        on_device, mesh=mesh, in_specs=in_specs, out_specs=out_specs, check_vma=False
    )
```

```python
import functools

import jax
import jax.numpy as jnp
from jax import lax
from jax.experimental import pallas as pl
from jax.experimental.pallas import tpu as pltpu
from jax.sharding import PartitionSpec as P

C = 256
DH = 128
EPS = 1e-06
BF = jnp.bfloat16
F32 = jnp.float32
VMEM_LIMIT = 36 << 20
CHUNKS = 4
STEP_BITS = (1, 3, 1, 3)


def dot_t(a, b):
    return lax.dot_general(a, b, (((1,), (1,)), ((), ())), preferred_element_type=F32)


def dot_tt(a, b):
    return lax.dot_general(a, b, (((0,), (0,)), ((), ())), preferred_element_type=F32)


def params():
    return pltpu.CompilerParams(vmem_limit_bytes=VMEM_LIMIT)


def cost(flops, nbytes):
    return pl.CostEstimate(flops=flops >> 12, bytes_accessed=nbytes >> 12, transcendentals=0)


def start_all(copies):
    for copy in copies:
        copy.start()
    return copies


def start_all(copies):
    for copy in copies:
        copy.start()
    return copies


def wait_all(copies):
    for copy in copies:
        copy.wait()


def slice_copies(chunks, s_ref, w_hbm, outs, sems, first):
    copies = []
    for n, (chunk, out) in enumerate(zip(chunks, outs)):
        rows, cols = out.shape
        start = (s_ref[0] * 2 + s_ref[1 + STEP_BITS[chunk]]) * rows
        src = w_hbm.at[pl.ds(pl.multiple_of(start, rows), rows), chunk * cols : (chunk + 1) * cols]
        copies.append(pltpu.make_async_copy(src, out, sems.at[first + n]))
    return copies


def state_kernel(
    s_ref, k_hbm, v_hbm, w_hbm, total_ref, local_ref, w0_ref, w1_hbm, k_buf, v_buf, acc, w1_buf, sems
):
    heads = total_ref.shape[0]
    copies = []
    for stretch in range(4):
        rows = slice(stretch * C, (stretch + 1) * C)
        copies.append(
            start_all(
                [
                    pltpu.make_async_copy(src.at[rows], dst.at[rows], sems.at[2 * stretch + n])
                    for n, (src, dst) in enumerate(((k_hbm, k_buf), (v_hbm, v_buf)))
                ]
            )
        )
    slices = start_all(slice_copies((0, 1), s_ref, w_hbm, (w0_ref, w1_buf), sems, 8))
    for stretch in range(4):
        rows = slice(stretch * C, (stretch + 1) * C)
        wait_all(copies[stretch])
        for head in range(heads):
            cols = slice(head * DH, (head + 1) * DH)
            state = dot_tt(v_buf[rows, cols], k_buf[rows, cols])
            if stretch == 0:
                acc[head] = state
                local_ref[head, 0] = state.astype(BF)
            elif stretch == 1:
                state = acc[head] + state
                acc[head] = state
                local_ref[head, 2] = state.astype(BF)
            elif stretch == 2:
                acc[head] = acc[head] + state
                local_ref[head, 1] = state.astype(BF)
            else:
                total_ref[head] = (acc[head] + state).astype(BF)
        if stretch == 1:
            wait_all(slices)
            store = pltpu.make_async_copy(w1_buf, w1_hbm, sems.at[10])
            store.start()
    store.wait()


def local_kernel(
    s_ref, q_hbm, k_hbm, v_hbm, w_hbm, g_ref, local_ref, token_ref, out_hbm, w2_hbm, w3_hbm,
    q_buf, k_buf, v_buf, out_buf, w2_buf, w3_buf, sems
):
    copies = []
    for stretch in range(4):
        rows = slice(stretch * C, (stretch + 1) * C)
        copies.append(
            start_all(
                [
                    pltpu.make_async_copy(src.at[rows], dst.at[rows], sems.at[3 * stretch + n])
                    for n, (src, dst) in enumerate(
                        ((q_hbm, q_buf), (k_hbm, k_buf), (v_hbm, v_buf))
                    )
                ]
            )
        )
    slices = start_all(slice_copies((2, 3), s_ref, w_hbm, (w2_buf, w3_buf), sems, 16))
    causal = lax.broadcasted_iota(jnp.int32, (C, C), 0) <= lax.broadcasted_iota(
        jnp.int32, (C, C), 1
    )
    stores = []
    for stretch in range(4):
        rows = slice(stretch * C, (stretch + 1) * C)
        wait_all(copies[stretch])
        for head in range(local_ref.shape[0]):
            cols = slice(head * DH, (head + 1) * DH)
            gate = lambda level: g_ref[level, head : head + 1, rows]
            q = q_buf[rows, cols]
            weights = jnp.where(causal, dot_t(k_buf[rows, cols], q), 0.0).astype(BF)
            out = dot_tt(v_buf[rows, cols], weights) * gate(0)
            if stretch % 2 == 1:
                out = out + dot_t(local_ref[head, stretch // 2], q) * gate(1)
            if stretch // 2 == 1:
                out = out + dot_t(local_ref[head, 2], q) * gate(2)
            out_buf[stretch, cols, :] = out
        store = pltpu.make_async_copy(
            out_buf.at[stretch], out_hbm.at[stretch], sems.at[12 + stretch]
        )
        store.start()
        stores.append(store)
        if stretch == 1:
            wait_all(slices)
            for n, (buf, out) in enumerate(((w2_buf, w2_hbm), (w3_buf, w3_hbm))):
                stores.append(pltpu.make_async_copy(buf, out, sems.at[18 + n]))
                stores[-1].start()
    wait_all(stores)


def far_block(s_ref, q_ref, comb_ref, g_ref, core_ref, zo_ref, yo_ref, zs_ref, ys_ref, out_ref):
    masks = [s_ref[1 + j].astype(F32) for j in range(5)]
    half = zo_ref.shape[1]
    for slot in range(2 * half):
        own = slot < half
        inner = slot % half
        head = (s_ref[0] if own else 1 - s_ref[0]) * half + inner
        z_ref, y_ref = (zo_ref, yo_ref) if own else (zs_ref, ys_ref)
        offset = pl.multiple_of(head * DH, DH)
        states = jnp.concatenate(
            [core_ref[head], z_ref[0, inner], z_ref[1, inner], y_ref[0, inner], y_ref[1, inner]], 0
        )
        read = dot_t(states, q_ref[:, pl.ds(offset, DH)])
        out = comb_ref[0, pl.ds(offset, DH), :]
        for j in range(5):
            out = out + read[j * DH : (j + 1) * DH] * (g_ref[3 + j, pl.ds(head, 1), :] * masks[j])
        mean = jnp.mean(out * out, axis=0, keepdims=True)
        out_ref[:, slot * DH : (slot + 1) * DH] = jnp.transpose(
            (out * lax.rsqrt(mean + EPS)).astype(BF)
        )


def far_first_kernel(s_ref, token_ref, *refs):
    far_block(s_ref, *refs)


def far_rest_kernel(s_ref, token_ref, *refs):
    *inputs, near_ref, keep_ref, buf = refs
    far_block(s_ref, *inputs, buf)

    @pl.when(pl.program_id(0) == 0)
    def _():
        near_ref[...] = buf[...]

    @pl.when(pl.program_id(0) > 0)
    def _():
        keep_ref[0] = buf[...]


def weight_copies(chunk, s_ref, w_hbm, pieces, dst, size, cols, sems, first):
    rows = dst.shape[0]
    half, quarter = rows // 4, rows // 8
    core, low = s_ref[0], s_ref[1 + STEP_BITS[chunk]]
    copies = []

    def add(src, row, count):
        copies.append(
            pltpu.make_async_copy(
                src, dst.at[pl.ds(row, count), cols], sems.at[first + len(copies)]
            )
        )

    own_cols = slice(chunk * size + cols.start, chunk * size + cols.stop)
    for part, which in enumerate((core, 1 - core)):
        add(w_hbm.at[pl.ds(pl.multiple_of(which * half, half), half), own_cols], part * half, half)
    for part, ref in enumerate(pieces):
        place = low if part % 2 == 0 else 1 - low
        start = pl.multiple_of((2 + part // 2) * half + place * quarter, quarter)
        add(ref.at[:, cols], start, quarter)
    return copies


def across_kernel(chunk, s_ref, token_ref, keep, got, w_hbm, *refs):
    pieces, out_ref, lhs, w, sems = refs[:4], *refs[4:]
    width = lhs.shape[1] // 2
    size = out_ref.shape[1]
    tile = size // 2
    left = start_all(
        [
            pltpu.make_async_copy(keep.at[0], lhs.at[:, :width], sems.at[0]),
            pltpu.make_async_copy(got, lhs.at[:, width:], sems.at[1]),
        ]
    )
    right = [
        start_all(
            weight_copies(
                chunk, s_ref, w_hbm, pieces, w, size, slice(n * tile, (n + 1) * tile), sems, 2 + 6 * n
            )
        )
        for n in range(2)
    ]
    wait_all(left)
    for n, group in enumerate(right):
        cols = slice(n * tile, (n + 1) * tile)
        wait_all(group)
        out_ref[:, cols] = jnp.dot(lhs[...], w[:, cols], preferred_element_type=F32).astype(
            out_ref.dtype
        )


def own_kernel(s_ref, token_ref, keep, got, w_hbm, *refs):
    count = CHUNKS
    pieces = [refs[4 * i : 4 * i + 4] for i in range(count)]
    received = refs[4 * count : 5 * count - 1]
    out_hbm, last_ref, lhs, w, out_buf, sems = refs[5 * count - 1 :]
    width = lhs.shape[1] // 2
    size = w.shape[2]
    left = start_all(
        [
            pltpu.make_async_copy(keep.at[1], lhs.at[:, :width], sems.at[0]),
            pltpu.make_async_copy(got, lhs.at[:, width:], sems.at[1]),
        ]
    )
    right = [
        start_all(
            weight_copies(
                i, s_ref, w_hbm, pieces[i], w.at[i], size, slice(0, size), sems, 2 + 6 * i
            )
        )
        for i in range(count)
    ]
    wait_all(left)
    stores = []
    for i in range(count):
        cols = slice(i * size, (i + 1) * size)
        wait_all(right[i])
        own = jnp.dot(lhs[...], w[i], preferred_element_type=F32)
        if i == count - 1:
            last_ref[...] = own
            break
        out_buf[:, cols] = (own + received[i][...].astype(F32)).astype(BF)
        store = pltpu.make_async_copy(
            out_buf.at[:, cols], out_hbm.at[:, cols], sems.at[2 + 6 * count + i]
        )
        store.start()
        stores.append(store)
    wait_all(stores)


def finish_kernel(base_ref, own_ref, got_ref, out_hbm, buf, sem):
    buf[...] = (own_ref[...] + got_ref[...].astype(F32)).astype(BF)
    size = buf.shape[1]
    copy = pltpu.make_async_copy(buf, out_hbm.at[:, (CHUNKS - 1) * size : CHUNKS * size], sem.at[0])
    copy.start()
    copy.wait()


def on_device(query_rows, key_rows, value_rows, level_gate, out_weight):
    tokens, width = query_rows.shape
    levels, heads, _ = level_gate.shape
    model = out_weight.shape[1]
    stretches = tokens // C
    half = heads // 2
    chunk = model // CHUNKS
    ctx_size = lax.axis_size("ctx")
    me = lax.axis_index("ctx")
    x = lax.axis_index("head")
    bit = lambda j: lax.bitwise_and(lax.shift_right_logical(me, j), 1)
    core = bit(0)
    any_spec = pl.BlockSpec(memory_space=pl.ANY)
    vmem_spec = pl.BlockSpec(memory_space=pltpu.VMEM)
    smem_spec = pl.BlockSpec(memory_space=pltpu.SMEM)
    dma = pltpu.SemaphoreType.DMA
    near_x, across_x, far_x = lax.bitwise_xor(x, 1), 3 - x, lax.bitwise_xor(x, 2)
    scalars = jnp.stack([core] + [bit(j) for j in range(5)] + [far_x, near_x, across_x, x])
    scalars = scalars.astype(jnp.int32)
    hbm = lambda array: pltpu.with_memory_space_constraint(array, pltpu.HBM)
    query_rows, key_rows, value_rows, out_weight = map(
        hbm, (query_rows, key_rows, value_rows, out_weight)
    )

    def ctx_swap(array, step):
        return lax.ppermute(array, "ctx", [(i, i ^ step) for i in range(ctx_size)])

    def near(array):
        return lax.ppermute(array, "head", [(i, i ^ 1) for i in range(4)])

    def across(array):
        return lax.ppermute(array, "head", [(i, 3 - i) for i in range(4)])

    def after(array, *tokens, space=jax.ShapeDtypeStruct):
        def kernel(*refs):
            pass

        return pl.pallas_call(
            kernel,
            in_specs=[any_spec] * (1 + len(tokens)),
            out_specs=any_spec,
            out_shape=space(array.shape, array.dtype),
            input_output_aliases={0: 0},
            name="after",
        )(array, *tokens)

    piece_shape = jax.ShapeDtypeStruct((width // 4, chunk), BF)
    total, local, slice0, slice1 = pl.pallas_call(
        state_kernel,
        in_specs=[smem_spec, any_spec, any_spec, any_spec],
        out_specs=[vmem_spec] * 3 + [any_spec],
        out_shape=[
            jax.ShapeDtypeStruct((heads, DH, DH), BF),
            jax.ShapeDtypeStruct((heads, 3, DH, DH), BF),
            piece_shape,
            pltpu.HBM((width // 4, chunk), BF),
        ],
        scratch_shapes=[
            pltpu.VMEM((tokens, width), BF),
            pltpu.VMEM((tokens, width), BF),
            pltpu.VMEM((heads, DH, DH), F32),
            pltpu.VMEM((width // 4, chunk), BF),
            dma((11,)),
        ],
        cost_estimate=cost(2 * tokens * width * DH, 7 << 20),
        compiler_params=params(),
        name="states",
    )(scalars, key_rows, value_rows, out_weight)

    pick = lambda array: lax.dynamic_slice_in_dim(array, core * half, half, 0)
    add = lambda *arrays: sum(a.astype(F32) for a in arrays)
    sibling = ctx_swap(total, 1)
    fetched = [near(slice0)]
    chip = add(pick(total), pick(sibling)).astype(BF)
    z1, z2, z3 = (ctx_swap(chip, step) for step in (2, 4, 6))
    fetched.append(near(after(slice1, chip, space=pltpu.HBM)))

    combined, slice2, slice3 = pl.pallas_call(
        local_kernel,
        in_specs=[smem_spec] + [any_spec] * 4 + [vmem_spec] * 2 + [any_spec],
        out_specs=[any_spec] * 3,
        out_shape=[pltpu.HBM((stretches, width, C), F32)] + [pltpu.HBM((width // 4, chunk), BF)] * 2,
        scratch_shapes=[
            pltpu.VMEM((tokens, width), BF),
            pltpu.VMEM((tokens, width), BF),
            pltpu.VMEM((tokens, width), BF),
            pltpu.VMEM((stretches, width, C), F32),
            pltpu.VMEM((width // 4, chunk), BF),
            pltpu.VMEM((width // 4, chunk), BF),
            dma((20,)),
        ],
        cost_estimate=cost(12 * tokens * width * DH, 12 << 20),
        compiler_params=params(),
        name="local",
    )(scalars, query_rows, key_rows, value_rows, out_weight, level_gate, local, chip)
    combined = hbm(combined)
    z3 = after(z3, combined)
    first_of_two = lax.broadcasted_iota(jnp.int32, (2, half, DH, DH), 0) == 0
    pair = lambda one, *two: jnp.where(first_of_two, one[None], add(*two).astype(BF)[None])
    z_own = pair(z1, z2, z3)
    row = add(chip, z1, z2, z3).astype(BF)
    y1, y2, y3 = (ctx_swap(row, step) for step in (8, 16, 24))
    z_sib = ctx_swap(z_own, 1)

    def gather(i, first_token, second_token):
        mine = after(fetched[i], first_token)
        other = after(ctx_swap(mine, 1 << STEP_BITS[i]), second_token)
        return (mine, other, ctx_swap(mine, 1), ctx_swap(other, 1))

    y_own = pair(y1, y2, y3)
    y_sib = ctx_swap(y_own, 1)
    fetched.append(near(after(slice2, z_own, space=pltpu.HBM)))
    pieces = [gather(0, z_own, y_own)]

    def far_norm(first, token):
        count = 1 if first else 3
        base = 6 if first else 7
        block = (C, width)
        full = lambda *shape: pl.BlockSpec(shape, lambda i, s: (0,) * len(shape))
        return pl.pallas_call(
            far_first_kernel if first else far_rest_kernel,
            grid_spec=pltpu.PrefetchScalarGridSpec(
                num_scalar_prefetch=1,
                grid=(count,),
                in_specs=[
                    any_spec,
                    pl.BlockSpec((C, width), lambda i, s: (s[base + i], 0)),
                    pl.BlockSpec((1, width, C), lambda i, s: (s[base + i], 0, 0)),
                    pl.BlockSpec((levels, heads, C), lambda i, s: (0, 0, s[base + i])),
                ]
                + [full(heads, DH, DH)] + [full(2, half, DH, DH)] * 4,
                out_specs=[pl.BlockSpec(block, lambda i, s: (0, 0))]
                + (
                    []
                    if first
                    else [pl.BlockSpec((1, *block), lambda i, s: (jnp.maximum(i - 1, 0), 0, 0))]
                ),
                scratch_shapes=[] if first else [pltpu.VMEM(block, BF)],
            ),
            out_shape=[pltpu.HBM(block, BF)] + ([] if first else [pltpu.HBM((2, *block), BF)]),
            cost_estimate=cost(10 * count * C * width * DH, count * (2 << 20)),
            compiler_params=params(),
            name="far_first" if first else "far_rest",
        )(
            scalars, token, query_rows, combined, level_gate, sibling, z_own, y_own, z_sib, y_sib
        )

    (first,) = far_norm(True, pieces[0][3])
    first = hbm(first)
    got_across = near(first)
    near_rows, keep = map(hbm, far_norm(False, first))

    def project(i, tokens):
        def kernel(s_ref, *refs):
            across_kernel(i, s_ref, *refs[len(tokens) - 1 :])

        return pl.pallas_call(
            kernel,
            in_specs=[smem_spec] + [any_spec] * (7 + len(tokens)),
            out_specs=vmem_spec,
            out_shape=jax.ShapeDtypeStruct((C, chunk), BF),
            scratch_shapes=[
                pltpu.VMEM((C, 2 * width), BF),
                pltpu.VMEM((2 * width, chunk), BF),
                dma((14,)),
            ],
            cost_estimate=cost(4 * C * width * chunk, 5 << 20),
            compiler_params=params(),
            name="across%d" % i,
        )(scalars, *tokens, keep, got_across, out_weight, *pieces[i])

    partials = [project(0, [keep])]
    received = [across(partials[0])]
    pieces.append(gather(1, y_own, keep))
    fetched.append(near(after(slice3, partials[0], space=pltpu.HBM)))
    pieces.append(gather(2, keep, partials[0]))
    partials.append(project(1, [partials[0]]))
    received.append(across(partials[1]))
    got_own = near(after(near_rows, partials[1]))
    partials.append(project(2, [partials[1], received[0]]))
    received.append(across(partials[2]))
    pieces.append(gather(3, partials[1], partials[2]))
    partials.append(project(3, [partials[2], received[1]]))
    received.append(across(partials[3]))
    token = partials[3]
    out, last = pl.pallas_call(
        own_kernel,
        in_specs=[smem_spec] + [any_spec] * (4 + 4 * CHUNKS) + [vmem_spec] * (CHUNKS - 1),
        out_specs=[any_spec, vmem_spec],
        out_shape=[pltpu.HBM((C, model), BF), jax.ShapeDtypeStruct((C, chunk), F32)],
        scratch_shapes=[
            pltpu.VMEM((C, 2 * width), BF),
            pltpu.VMEM((CHUNKS, 2 * width, chunk), BF),
            pltpu.VMEM((C, (CHUNKS - 1) * chunk), BF),
            dma((2 + 7 * CHUNKS,)),
        ],
        cost_estimate=cost(4 * C * width * model, 20 << 20),
        compiler_params=params(),
        name="own",
    )(
        scalars,
        token,
        keep,
        got_own,
        out_weight,
        *[piece for group in pieces for piece in group],
        *received[:-1],
    )
    return pl.pallas_call(
        finish_kernel,
        in_specs=[any_spec, vmem_spec, vmem_spec],
        out_specs=any_spec,
        out_shape=pltpu.HBM((C, model), BF),
        scratch_shapes=[pltpu.VMEM((C, chunk), BF), dma((1,))],
        input_output_aliases={0: 0},
        compiler_params=params(),
        name="finish",
    )(out, last, received[-1])


def solution(mesh):
    in_specs = (
        P("ctx", "head"),
        P("ctx", "head"),
        P("ctx", "head"),
        P(None, "head", "ctx"),
        P("head", None),
    )
    out_specs = P(("ctx", "head"), None)
    return jax.shard_map(
        on_device, mesh=mesh, in_specs=in_specs, out_specs=out_specs, check_vma=False
    )
```

```python
import functools

import jax
import jax.numpy as jnp
from jax import lax
from jax.experimental import pallas as pl
from jax.experimental.pallas import tpu as pltpu
from jax.sharding import PartitionSpec as P

C = 256
DH = 128
EPS = 1e-06
BF = jnp.bfloat16
F32 = jnp.float32
VMEM_LIMIT = 36 << 20
CHUNKS = 4
STEP_BITS = (1, 3, 1, 3)


def dot_t(a, b):
    return lax.dot_general(a, b, (((1,), (1,)), ((), ())), preferred_element_type=F32)


def dot_tt(a, b):
    return lax.dot_general(a, b, (((0,), (0,)), ((), ())), preferred_element_type=F32)


def params():
    return pltpu.CompilerParams(vmem_limit_bytes=VMEM_LIMIT)


def cost(flops, nbytes):
    return pl.CostEstimate(flops=flops >> 12, bytes_accessed=nbytes >> 12, transcendentals=0)


def start_all(copies):
    for copy in copies:
        copy.start()
    return copies


def start_all(copies):
    for copy in copies:
        copy.start()
    return copies


def wait_all(copies):
    for copy in copies:
        copy.wait()


def slice_copies(chunks, s_ref, w_hbm, outs, sems, first):
    copies = []
    for n, (chunk, out) in enumerate(zip(chunks, outs)):
        rows, cols = out.shape
        start = (s_ref[0] * 2 + s_ref[1 + STEP_BITS[chunk]]) * rows
        src = w_hbm.at[pl.ds(pl.multiple_of(start, rows), rows), chunk * cols : (chunk + 1) * cols]
        copies.append(pltpu.make_async_copy(src, out, sems.at[first + n]))
    return copies


def state_kernel(
    s_ref, k_hbm, v_hbm, w_hbm, total_ref, local_ref, w0_hbm, w1_hbm, k_buf, v_buf, acc, sems
):
    heads = total_ref.shape[0]
    copies = []
    for stretch in range(4):
        rows = slice(stretch * C, (stretch + 1) * C)
        copies.append(
            start_all(
                [
                    pltpu.make_async_copy(src.at[rows], dst.at[rows], sems.at[2 * stretch + n])
                    for n, (src, dst) in enumerate(((k_hbm, k_buf), (v_hbm, v_buf)))
                ]
            )
        )
    slices = start_all(slice_copies((0, 1), s_ref, w_hbm, (w0_hbm, w1_hbm), sems, 8))
    for stretch in range(4):
        rows = slice(stretch * C, (stretch + 1) * C)
        wait_all(copies[stretch])
        for head in range(heads):
            cols = slice(head * DH, (head + 1) * DH)
            state = dot_tt(v_buf[rows, cols], k_buf[rows, cols])
            if stretch == 0:
                acc[head] = state
                local_ref[head, 0] = state.astype(BF)
            elif stretch == 1:
                state = acc[head] + state
                acc[head] = state
                local_ref[head, 2] = state.astype(BF)
            elif stretch == 2:
                acc[head] = acc[head] + state
                local_ref[head, 1] = state.astype(BF)
            else:
                total_ref[head] = (acc[head] + state).astype(BF)
    wait_all(slices)


def local_kernel(
    s_ref, q_hbm, k_hbm, v_hbm, w_hbm, g_ref, local_ref, token_ref, out_hbm, w2_ref, w3_ref,
    q_buf, k_buf, v_buf, out_buf, sems
):
    copies = []
    for stretch in range(4):
        rows = slice(stretch * C, (stretch + 1) * C)
        copies.append(
            start_all(
                [
                    pltpu.make_async_copy(src.at[rows], dst.at[rows], sems.at[3 * stretch + n])
                    for n, (src, dst) in enumerate(
                        ((q_hbm, q_buf), (k_hbm, k_buf), (v_hbm, v_buf))
                    )
                ]
            )
        )
    slices = start_all(slice_copies((2, 3), s_ref, w_hbm, (w2_ref, w3_ref), sems, 16))
    causal = lax.broadcasted_iota(jnp.int32, (C, C), 0) <= lax.broadcasted_iota(
        jnp.int32, (C, C), 1
    )
    stores = []
    for stretch in range(4):
        rows = slice(stretch * C, (stretch + 1) * C)
        wait_all(copies[stretch])
        for head in range(local_ref.shape[0]):
            cols = slice(head * DH, (head + 1) * DH)
            gate = lambda level: g_ref[level, head : head + 1, rows]
            q = q_buf[rows, cols]
            weights = jnp.where(causal, dot_t(k_buf[rows, cols], q), 0.0).astype(BF)
            out = dot_tt(v_buf[rows, cols], weights) * gate(0)
            if stretch % 2 == 1:
                out = out + dot_t(local_ref[head, stretch // 2], q) * gate(1)
            if stretch // 2 == 1:
                out = out + dot_t(local_ref[head, 2], q) * gate(2)
            out_buf[stretch, cols, :] = out
        store = pltpu.make_async_copy(
            out_buf.at[stretch], out_hbm.at[stretch], sems.at[12 + stretch]
        )
        store.start()
        stores.append(store)
    wait_all(stores)
    wait_all(slices)


def far_block(s_ref, q_ref, comb_ref, g_ref, core_ref, zo_ref, yo_ref, zs_ref, ys_ref, out_ref):
    masks = [s_ref[1 + j].astype(F32) for j in range(5)]
    half = zo_ref.shape[1]
    for slot in range(2 * half):
        own = slot < half
        inner = slot % half
        head = (s_ref[0] if own else 1 - s_ref[0]) * half + inner
        z_ref, y_ref = (zo_ref, yo_ref) if own else (zs_ref, ys_ref)
        offset = pl.multiple_of(head * DH, DH)
        states = jnp.concatenate(
            [core_ref[head], z_ref[0, inner], z_ref[1, inner], y_ref[0, inner], y_ref[1, inner]], 0
        )
        read = dot_t(states, q_ref[:, pl.ds(offset, DH)])
        out = comb_ref[0, pl.ds(offset, DH), :]
        for j in range(5):
            out = out + read[j * DH : (j + 1) * DH] * (g_ref[3 + j, pl.ds(head, 1), :] * masks[j])
        mean = jnp.mean(out * out, axis=0, keepdims=True)
        out_ref[:, slot * DH : (slot + 1) * DH] = jnp.transpose(
            (out * lax.rsqrt(mean + EPS)).astype(BF)
        )


def far_first_kernel(s_ref, token_ref, *refs):
    far_block(s_ref, *refs)


def far_rest_kernel(s_ref, token_ref, *refs):
    *inputs, near_ref, keep_ref, buf = refs
    far_block(s_ref, *inputs, buf)

    @pl.when(pl.program_id(0) == 0)
    def _():
        near_ref[...] = buf[...]

    @pl.when(pl.program_id(0) > 0)
    def _():
        keep_ref[0] = buf[...]


def gate_kernel(data_ref, token_ref, out_ref):
    pass


def weight_copies(chunk, s_ref, w_hbm, pieces, dst, size, cols, sems, first):
    rows = dst.shape[0]
    half, quarter = rows // 4, rows // 8
    core, low = s_ref[0], s_ref[1 + STEP_BITS[chunk]]
    copies = []

    def add(src, row, count):
        copies.append(
            pltpu.make_async_copy(
                src, dst.at[pl.ds(row, count), cols], sems.at[first + len(copies)]
            )
        )

    own_cols = slice(chunk * size + cols.start, chunk * size + cols.stop)
    for part, which in enumerate((core, 1 - core)):
        add(w_hbm.at[pl.ds(pl.multiple_of(which * half, half), half), own_cols], part * half, half)
    for part, ref in enumerate(pieces):
        place = low if part % 2 == 0 else 1 - low
        start = pl.multiple_of((2 + part // 2) * half + place * quarter, quarter)
        add(ref.at[:, cols], start, quarter)
    return copies


def across_kernel(chunk, s_ref, token_ref, keep, got, w_hbm, *refs):
    pieces, out_ref, lhs, w, sems = refs[:4], *refs[4:]
    width = lhs.shape[1] // 2
    size = out_ref.shape[1]
    tile = size // 2
    left = start_all(
        [
            pltpu.make_async_copy(keep.at[0], lhs.at[:, :width], sems.at[0]),
            pltpu.make_async_copy(got, lhs.at[:, width:], sems.at[1]),
        ]
    )
    right = [
        start_all(
            weight_copies(
                chunk, s_ref, w_hbm, pieces, w, size, slice(n * tile, (n + 1) * tile), sems, 2 + 6 * n
            )
        )
        for n in range(2)
    ]
    wait_all(left)
    for n, group in enumerate(right):
        cols = slice(n * tile, (n + 1) * tile)
        wait_all(group)
        out_ref[:, cols] = jnp.dot(lhs[...], w[:, cols], preferred_element_type=F32).astype(
            out_ref.dtype
        )


def own_kernel(s_ref, token_ref, keep, got, w_hbm, *refs):
    count = CHUNKS
    pieces = [refs[4 * i : 4 * i + 4] for i in range(count)]
    received = refs[4 * count : 5 * count - 1]
    out_hbm, last_ref, lhs, w, out_buf, sems = refs[5 * count - 1 :]
    width = lhs.shape[1] // 2
    size = w.shape[2]
    left = start_all(
        [
            pltpu.make_async_copy(keep.at[1], lhs.at[:, :width], sems.at[0]),
            pltpu.make_async_copy(got, lhs.at[:, width:], sems.at[1]),
        ]
    )
    right = [
        start_all(
            weight_copies(
                i, s_ref, w_hbm, pieces[i], w.at[i], size, slice(0, size), sems, 2 + 6 * i
            )
        )
        for i in range(count)
    ]
    wait_all(left)
    stores = []
    for i in range(count):
        cols = slice(i * size, (i + 1) * size)
        wait_all(right[i])
        own = jnp.dot(lhs[...], w[i], preferred_element_type=F32)
        if i == count - 1:
            last_ref[...] = own
            break
        out_buf[:, cols] = (own + received[i][...].astype(F32)).astype(BF)
        store = pltpu.make_async_copy(
            out_buf.at[:, cols], out_hbm.at[:, cols], sems.at[2 + 6 * count + i]
        )
        store.start()
        stores.append(store)
    wait_all(stores)


def finish_kernel(base_ref, own_ref, got_ref, out_hbm, buf, sem):
    buf[...] = (own_ref[...] + got_ref[...].astype(F32)).astype(BF)
    size = buf.shape[1]
    copy = pltpu.make_async_copy(buf, out_hbm.at[:, (CHUNKS - 1) * size : CHUNKS * size], sem.at[0])
    copy.start()
    copy.wait()


def on_device(query_rows, key_rows, value_rows, level_gate, out_weight):
    tokens, width = query_rows.shape
    levels, heads, _ = level_gate.shape
    model = out_weight.shape[1]
    stretches = tokens // C
    half = heads // 2
    chunk = model // CHUNKS
    ctx_size = lax.axis_size("ctx")
    me = lax.axis_index("ctx")
    x = lax.axis_index("head")
    bit = lambda j: lax.bitwise_and(lax.shift_right_logical(me, j), 1)
    core = bit(0)
    any_spec = pl.BlockSpec(memory_space=pl.ANY)
    vmem_spec = pl.BlockSpec(memory_space=pltpu.VMEM)
    smem_spec = pl.BlockSpec(memory_space=pltpu.SMEM)
    dma = pltpu.SemaphoreType.DMA
    near_x, across_x, far_x = lax.bitwise_xor(x, 1), 3 - x, lax.bitwise_xor(x, 2)
    scalars = jnp.stack([core] + [bit(j) for j in range(5)] + [far_x, near_x, across_x, x])
    scalars = scalars.astype(jnp.int32)
    hbm = lambda array: pltpu.with_memory_space_constraint(array, pltpu.HBM)
    query_rows, key_rows, value_rows, out_weight = map(
        hbm, (query_rows, key_rows, value_rows, out_weight)
    )

    def ctx_swap(array, step):
        return lax.ppermute(array, "ctx", [(i, i ^ step) for i in range(ctx_size)])

    def near(array):
        return lax.ppermute(array, "head", [(i, i ^ 1) for i in range(4)])

    def across(array):
        return lax.ppermute(array, "head", [(i, 3 - i) for i in range(4)])

    def after(array, token):
        return pl.pallas_call(
            gate_kernel,
            in_specs=[any_spec, any_spec],
            out_specs=any_spec,
            out_shape=jax.ShapeDtypeStruct(array.shape, array.dtype),
            input_output_aliases={0: 0},
            name="after",
        )(array, token)

    piece_shape = jax.ShapeDtypeStruct((width // 4, chunk), BF)
    total, local, slice0, slice1 = pl.pallas_call(
        state_kernel,
        in_specs=[smem_spec, any_spec, any_spec, any_spec],
        out_specs=[vmem_spec] * 4,
        out_shape=[
            jax.ShapeDtypeStruct((heads, DH, DH), BF),
            jax.ShapeDtypeStruct((heads, 3, DH, DH), BF),
            piece_shape,
            piece_shape,
        ],
        scratch_shapes=[
            pltpu.VMEM((tokens, width), BF),
            pltpu.VMEM((tokens, width), BF),
            pltpu.VMEM((heads, DH, DH), F32),
            dma((10,)),
        ],
        cost_estimate=cost(2 * tokens * width * DH, 7 << 20),
        compiler_params=params(),
        name="states",
    )(scalars, key_rows, value_rows, out_weight)

    pick = lambda array: lax.dynamic_slice_in_dim(array, core * half, half, 0)
    add = lambda *arrays: sum(a.astype(F32) for a in arrays)
    sibling = ctx_swap(total, 1)
    fetched = [near(slice0)]
    chip = add(pick(total), pick(sibling)).astype(BF)
    z1, z2, z3 = (ctx_swap(chip, step) for step in (2, 4, 6))
    fetched.append(near(after(slice1, chip)))

    combined, slice2, slice3 = pl.pallas_call(
        local_kernel,
        in_specs=[smem_spec] + [any_spec] * 4 + [vmem_spec] * 2 + [any_spec],
        out_specs=[any_spec, vmem_spec, vmem_spec],
        out_shape=[pltpu.HBM((stretches, width, C), F32), piece_shape, piece_shape],
        scratch_shapes=[
            pltpu.VMEM((tokens, width), BF),
            pltpu.VMEM((tokens, width), BF),
            pltpu.VMEM((tokens, width), BF),
            pltpu.VMEM((stretches, width, C), F32),
            dma((18,)),
        ],
        cost_estimate=cost(12 * tokens * width * DH, 12 << 20),
        compiler_params=params(),
        name="local",
    )(scalars, query_rows, key_rows, value_rows, out_weight, level_gate, local, chip)
    combined = hbm(combined)
    z3 = after(z3, combined)
    z_own = jnp.stack([z1, add(z2, z3).astype(BF)])
    row = add(chip, z1, z2, z3).astype(BF)
    y1, y2, y3 = (ctx_swap(row, step) for step in (8, 16, 24))
    z_sib = ctx_swap(z_own, 1)

    def gather(i, first_token, second_token):
        mine = after(fetched[i], first_token)
        other = after(ctx_swap(mine, 1 << STEP_BITS[i]), second_token)
        return (mine, other, ctx_swap(mine, 1), ctx_swap(other, 1))

    y_own = jnp.stack([y1, add(y2, y3).astype(BF)])
    y_sib = ctx_swap(y_own, 1)
    fetched.append(near(after(slice2, z_own)))
    pieces = [gather(0, z_own, y_own)]

    def far_norm(first, token):
        count = 1 if first else 3
        base = 6 if first else 7
        block = (C, width)
        full = lambda *shape: pl.BlockSpec(shape, lambda i, s: (0,) * len(shape))
        return pl.pallas_call(
            far_first_kernel if first else far_rest_kernel,
            grid_spec=pltpu.PrefetchScalarGridSpec(
                num_scalar_prefetch=1,
                grid=(count,),
                in_specs=[
                    any_spec,
                    pl.BlockSpec((C, width), lambda i, s: (s[base + i], 0)),
                    pl.BlockSpec((1, width, C), lambda i, s: (s[base + i], 0, 0)),
                    pl.BlockSpec((levels, heads, C), lambda i, s: (0, 0, s[base + i])),
                ]
                + [full(heads, DH, DH)] + [full(2, half, DH, DH)] * 4,
                out_specs=[pl.BlockSpec(block, lambda i, s: (0, 0))]
                + (
                    []
                    if first
                    else [pl.BlockSpec((1, *block), lambda i, s: (jnp.maximum(i - 1, 0), 0, 0))]
                ),
                scratch_shapes=[] if first else [pltpu.VMEM(block, BF)],
            ),
            out_shape=[pltpu.HBM(block, BF)] + ([] if first else [pltpu.HBM((2, *block), BF)]),
            cost_estimate=cost(10 * count * C * width * DH, count * (2 << 20)),
            compiler_params=params(),
            name="far_first" if first else "far_rest",
        )(
            scalars, token, query_rows, combined, level_gate, sibling, z_own, y_own, z_sib, y_sib
        )

    (first,) = far_norm(True, y_own)
    first = hbm(first)
    got_across = near(first)
    near_rows, keep = map(hbm, far_norm(False, first))

    def project(i, tokens):
        def kernel(s_ref, *refs):
            across_kernel(i, s_ref, *refs[len(tokens) - 1 :])

        return pl.pallas_call(
            kernel,
            in_specs=[smem_spec] + [any_spec] * (7 + len(tokens)),
            out_specs=vmem_spec,
            out_shape=jax.ShapeDtypeStruct((C, chunk), BF),
            scratch_shapes=[
                pltpu.VMEM((C, 2 * width), BF),
                pltpu.VMEM((2 * width, chunk), BF),
                dma((14,)),
            ],
            cost_estimate=cost(4 * C * width * chunk, 5 << 20),
            compiler_params=params(),
            name="across%d" % i,
        )(scalars, *tokens, keep, got_across, out_weight, *pieces[i])

    partials = [project(0, [keep])]
    received = [across(partials[0])]
    pieces.append(gather(1, y_own, keep))
    fetched.append(near(after(slice3, partials[0])))
    pieces.append(gather(2, keep, partials[0]))
    partials.append(project(1, [partials[0]]))
    received.append(across(partials[1]))
    got_own = near(after(near_rows, partials[1]))
    partials.append(project(2, [partials[1], received[0]]))
    received.append(across(partials[2]))
    pieces.append(gather(3, partials[1], partials[2]))
    partials.append(project(3, [partials[2], received[1]]))
    received.append(across(partials[3]))
    token = partials[3]
    out, last = pl.pallas_call(
        own_kernel,
        in_specs=[smem_spec] + [any_spec] * (4 + 4 * CHUNKS) + [vmem_spec] * (CHUNKS - 1),
        out_specs=[any_spec, vmem_spec],
        out_shape=[pltpu.HBM((C, model), BF), jax.ShapeDtypeStruct((C, chunk), F32)],
        scratch_shapes=[
            pltpu.VMEM((C, 2 * width), BF),
            pltpu.VMEM((CHUNKS, 2 * width, chunk), BF),
            pltpu.VMEM((C, (CHUNKS - 1) * chunk), BF),
            dma((2 + 7 * CHUNKS,)),
        ],
        cost_estimate=cost(4 * C * width * model, 20 << 20),
        compiler_params=params(),
        name="own",
    )(
        scalars,
        token,
        keep,
        got_own,
        out_weight,
        *[piece for group in pieces for piece in group],
        *received[:-1],
    )
    return pl.pallas_call(
        finish_kernel,
        in_specs=[any_spec, vmem_spec, vmem_spec],
        out_specs=any_spec,
        out_shape=pltpu.HBM((C, model), BF),
        scratch_shapes=[pltpu.VMEM((C, chunk), BF), dma((1,))],
        input_output_aliases={0: 0},
        compiler_params=params(),
        name="finish",
    )(out, last, received[-1])


def solution(mesh):
    in_specs = (
        P("ctx", "head"),
        P("ctx", "head"),
        P("ctx", "head"),
        P(None, "head", "ctx"),
        P("head", None),
    )
    out_specs = P(("ctx", "head"), None)
    return jax.shard_map(
        on_device, mesh=mesh, in_specs=in_specs, out_specs=out_specs, check_vma=False
    )
```
